256 devices in a mesh: band: 16 (over z, core), gvec: 16 (over y, x).
Axes of the slice: x: 4, y: 4, z: 8, core: 2. Of those that a mesh axis runs over, the one named last changes fastest.
Arguments:
- pair_density: bfloat16 [768, 16, 60000], P('band', None, 'gvec'), may hold values from -6 to 6
- eigvecs: bfloat16 [60000, 2000], P('gvec', 'band'), may hold values from -0.0234375 to 0.0234375
- subspace: bfloat16 [4, 2000, 2000], P(None, 'gvec'), may hold values from -0.125 to 0.125
- counts: int32 [16], P('band'), may hold values from 1 to 48, as said below
- freq_index: int32 [768, 16], P('band'), may hold values from 0 to 3
- band_weight: float32 [768], P('band'), may hold values from 0.3 to 3
Outputs:
- coef: float32 [768, 16, 2000], P('band', None, 'gvec')
- sigma: float32 [16], replicated
The draws below stay inside these ranges and needn't reach their ends.
Inputs may be any that keep to these rules, and one draw needn't show every extreme that they name: `counts`: each group has at least one live slot; some group has all 48 slots live.
All inputs are finite; a program needn't handle non-finite values.
Results may differ from the reference program's by a relative error of at most 0.0026.
Values may be sent and summed in bfloat16 or wider, within the bound.
No kernel may reach another device: no remote copies, remote signals or barrier semaphores. Data moves between devices by JAX's collectives and lax.ppermute only.
A program may use at most 128 MiB of HBM per device.

```python
import math
import jax
import jax.numpy as jnp
from jax import lax

NG = 60000
NEIG = 2000
NW = 4
CAP = 48
NM = 16
NGROUP = 16


def draw_counts(key, part):
    key = jax.random.fold_in(key, 11)
    key_jitter, key_full = jax.random.split(key)
    group = jnp.arange(NGROUP, dtype=jnp.int32)
    spread = max(NGROUP - 1, 1)
    base = CAP // 8 + 7 * CAP * group * group // (8 * spread * spread)
    jitter = jax.random.randint(key_jitter, (NGROUP,), -(CAP // 16), CAP // 16 + 1)
    number = jnp.clip(base + jitter, 1, CAP)
    chosen = jax.random.randint(key_full, (), 0, NGROUP)
    return jnp.where(group == chosen, CAP, number).astype(jnp.int32)


def place_ends(result, key, least, largest):
    longest = result.shape.index(max(result.shape))
    spots = []
    for shift in (0, 1):
        where = [jax.random.randint(jax.random.fold_in(key, axis), (), 0, length) for axis, length in enumerate(result.shape)]
        where[longest] = (where[longest] + shift) % result.shape[longest]
        spots.append(tuple(where))
    return result.at[spots[0]].set(least).at[spots[1]].set(largest)


def shard_levels(rng, extent, cuts, low, largest):
    factor_of = 1.0
    for dim, parts in cuts:
        steps = jax.random.uniform(jax.random.fold_in(jax.random.fold_in(rng, 6), dim), (parts,), jnp.float32, low / len(cuts), largest / len(cuts))
        factor_of = factor_of * jnp.repeat(jnp.exp(steps), extent[dim] // parts).reshape((-1,) + (1,) * (len(extent) - 1 - dim))
    return factor_of


def noise(own_key, dims, deviation, most, cuts=(), held_as=jnp.bfloat16):
    level = shard_levels(own_key, dims, cuts, -0.22, 0.18) if cuts else 1.0
    values = jax.random.normal(own_key, dims, jnp.float32) * deviation * level
    return jnp.minimum(jnp.maximum(values, -most), most).astype(held_as)


def setup_inputs(seed: int = 0) -> dict:
    arg_keys = jax.random.split(jax.random.key(seed), 7)
    pair_density = noise(arg_keys[0], (NGROUP * CAP, NM, NG), 1.0, 6.0, ((0, 16), (2, 16)))
    eigvecs = noise(arg_keys[1], (NG, NEIG), NG ** -0.5, 0.0234375, ((0, 16), (1, 16)))
    subspace = noise(arg_keys[2], (NW, NEIG, NEIG), NEIG ** -0.5, 0.125, ((1, 16),))
    counts = draw_counts(jax.random.fold_in(arg_keys[6], 71), 0)
    freq_index = place_ends(jax.random.randint(arg_keys[4], (NGROUP * CAP, NM), 0, NW), jax.random.fold_in(arg_keys[4], 1), 0, NW - 1).astype(jnp.int32)
    band_weight = jnp.clip(jnp.exp(math.log(3.0) - 2.3025851 * jax.random.uniform(arg_keys[5], (NGROUP * CAP,), jnp.float32) ** shard_levels(arg_keys[5], (NGROUP * CAP,), ((0, 16),), -0.2, 0.2)), 0.3, 3.0)
    return dict(pair_density=pair_density, eigvecs=eigvecs, subspace=subspace, counts=counts, freq_index=freq_index, band_weight=band_weight)


def reference(pair_density, eigvecs, subspace, counts, freq_index, band_weight):
    slot_ids = jnp.arange(CAP, dtype=jnp.int32)
    live = (slot_ids[None, :] < counts[:, None]).astype(jnp.float32).reshape(-1)
    grouped = pair_density.reshape(NGROUP, CAP * NM, NG)

    def project(block):
        return jnp.dot(block, eigvecs, preferred_element_type=jnp.float32)
    coef = lax.map(project, grouped).reshape(NGROUP * CAP, NM, NEIG)
    coef = coef * live[:, None, None]
    rounded = coef.astype(jnp.bfloat16).reshape(NGROUP * CAP * NM, NEIG)
    widened = rounded.astype(jnp.float32)

    def quadratic(matrix):
        applied = jnp.dot(rounded, matrix.T, preferred_element_type=jnp.float32)
        return lax.optimization_barrier(jnp.sum(widened * applied, axis=1))
    quad = lax.map(quadratic, subspace)
    nodes = jnp.arange(NW, dtype=jnp.int32)
    chosen = freq_index.reshape(-1)[None, :] == nodes[:, None]
    picked = lax.optimization_barrier(jnp.sum(jnp.where(chosen, quad, jnp.float32(0.0)), axis=0))
    weights = (band_weight * live)[:, None]
    total = lax.optimization_barrier(jnp.sum(picked.reshape(NGROUP * CAP, NM) * weights, axis=0))
    sigma = -total / jnp.float32(math.sqrt(NEIG * NGROUP * CAP))
    return (coef, sigma)
```

```python
import math

import jax
import jax.numpy as jnp
from jax import lax
from jax.experimental import pallas as pl
from jax.experimental.pallas import tpu as pltpu
from jax.sharding import PartitionSpec as P

NEIG = 2000
LANES = 128
LIMIT = 32000.0
STEPS = 24
SIDE = 4
HALF = 1872
VMEM = 48 * 1024 * 1024


def project_kernel(layout, cols, pd_ref, *refs):
    pieces, out_ref, rhs = refs[: len(layout)], refs[-2], refs[-1]

    @pl.when(pl.program_id(0) == 0)
    def _():
        for piece, (row, lane) in zip(pieces, layout):
            rhs[row : row + piece.shape[0], lane : lane + LANES] = piece[...]

    total = jnp.dot(pd_ref[...], rhs[...], preferred_element_type=jnp.float32)
    most = jnp.max(jnp.abs(total), axis=1, keepdims=True)
    scale = jnp.ones_like(most)
    power = jnp.zeros(most.shape, jnp.int32)
    for i in range(1, STEPS + 1):
        fits = most * float(2**i) <= LIMIT
        scale = jnp.where(fits, float(2**i), scale)
        power = jnp.where(fits, i, power)
    code = jnp.round(total * scale).astype(jnp.int32).astype(jnp.int16)
    parts, rows = out_ref.shape[:2]
    out_ref[:, :, 0:cols] = code.reshape(parts, rows, cols)
    wide = jnp.broadcast_to(power, (power.shape[0], LANES)).astype(jnp.int16)
    out_ref[:, :, cols : cols + LANES] = wide.reshape(parts, rows, LANES)


def project(flat, pieces, layout, cols, devices):
    nrows, depth = flat.shape
    split = 2
    block = nrows // split
    share = nrows // devices
    return pl.pallas_call(
        lambda *refs: project_kernel(layout, cols, *refs),
        grid=(split,),
        in_specs=[pl.BlockSpec((block, depth), lambda i: (i, 0))]
        + [pl.BlockSpec(p.shape, lambda i: (0, 0)) for p in pieces],
        out_specs=pl.BlockSpec((devices // split, share, cols + LANES), lambda i: (i, 0, 0)),
        out_shape=jax.ShapeDtypeStruct((devices, share, cols + LANES), jnp.int16),
        scratch_shapes=[pltpu.VMEM((depth, cols), jnp.bfloat16)],
        compiler_params=pltpu.CompilerParams(vmem_limit_bytes=VMEM),
        cost_estimate=pl.CostEstimate(
            flops=2 * nrows * depth * cols, bytes_accessed=2 * nrows * depth + 2 * depth * cols, transcendentals=0
        ),
        name="project",
    )(flat, *pieces)


def collect_kernel(code_ref, live_ref, coef_ref, rounded_ref):
    devices, rows, width = code_ref.shape
    cols = width - LANES
    total = jnp.zeros((rows, cols), jnp.float32)
    for d in range(devices):
        power = code_ref[d, :, cols : cols + LANES].astype(jnp.int32)[:, 0:1]
        unit = 1.0 / (jnp.ones_like(power) << power).astype(jnp.float32)
        total += code_ref[d, :, 0:cols].astype(jnp.int32).astype(jnp.float32) * unit
    total = total * live_ref[...]
    for n in range(cols // LANES):
        part = total[:, n * LANES : (n + 1) * LANES]
        coef_ref[n] = part
        rounded_ref[n] = part.astype(jnp.bfloat16)


def collect(code, live_rows):
    devices, rows, width = code.shape
    blocks = (width - LANES) // LANES
    return pl.pallas_call(
        collect_kernel,
        out_shape=(
            jax.ShapeDtypeStruct((blocks, rows, LANES), jnp.float32),
            jax.ShapeDtypeStruct((blocks, rows, LANES), jnp.bfloat16),
        ),
        compiler_params=pltpu.CompilerParams(vmem_limit_bytes=VMEM),
        name="collect",
    )(code, live_rows)


def quad_kernel(share, place_ref, own_ref, w_ref, pick_ref, coef_ref, *refs):
    pieces, out_ref, flat = refs[:SIDE], refs[SIDE], refs[SIDE + 1]
    rows = pieces[0].shape[1]
    blocks = pieces[0].shape[0]
    for k in range(blocks):
        at = place_ref[k]
        out_ref[k, 0:rows, :] = coef_ref[at]
        for d, piece in enumerate(pieces):
            flat[d * rows : (d + 1) * rows, k * share : (k + 1) * share] = piece[at][:, 0:share]
    total = jnp.zeros((SIDE * rows, 1), jnp.float32)
    for p in range(SIDE):
        at = own_ref[p]
        left = jnp.concatenate([piece[at] for piece in pieces], axis=0)[:, 0:share].astype(jnp.float32)
        for node in range(w_ref.shape[1]):
            applied = lax.dot_general(
                flat[...], w_ref[p, node], (((1,), (1,)), ((), ())), preferred_element_type=jnp.float32
            )
            total += jnp.sum(left * applied, axis=1, keepdims=True) * pick_ref[node]
    states = 16
    terms = jnp.sum(total.reshape(SIDE * rows // states, states, 1), axis=0)
    wide = jnp.broadcast_to(terms, (states, LANES))
    for k in range(blocks):
        out_ref[k, rows : rows + states, :] = wide


def quadratic(place, own, gathered, pick, coef, pieces, share):
    blocks, rows, _ = pieces[0].shape
    smem = pl.BlockSpec(memory_space=pltpu.SMEM)
    vmem = pl.BlockSpec(memory_space=pltpu.VMEM)
    return pl.pallas_call(
        lambda *refs: quad_kernel(share, *refs),
        in_specs=[smem, smem] + [vmem] * (3 + SIDE),
        out_specs=vmem,
        out_shape=jax.ShapeDtypeStruct((blocks, rows + 16, LANES), jnp.float32),
        scratch_shapes=[pltpu.VMEM((SIDE * rows, blocks * share), jnp.bfloat16)],
        compiler_params=pltpu.CompilerParams(vmem_limit_bytes=VMEM),
        name="quad",
    )(place, own, gathered, pick, coef, *pieces)


def local(pair_density, eigvecs, subspace, counts, freq_index, band_weight):
    slots, states, depth = pair_density.shape
    nodes, share, neig = subspace.shape
    devices = lax.axis_size("gvec")
    bands = lax.axis_size("band")
    chips = bands // 2
    nrows = slots * states
    rows = nrows // devices
    band, gvec = lax.axis_index("band"), lax.axis_index("gvec")
    zed, core = band >> 1, band & 1
    why, ex = gvec >> 2, gvec & 3

    def shift(value, by):
        return lax.ppermute(value, "band", [(b, (b + 2 * by) % bands) for b in range(bands)])

    def sibling(value):
        return lax.ppermute(value, "band", [(b, b ^ 1) for b in range(bands)])

    def along_y(value, by):
        return lax.ppermute(value, "gvec", [(g, (g + SIDE * by) % devices) for g in range(devices)])

    flat = pair_density.reshape(nrows, depth)
    mine = jnp.pad(eigvecs, ((0, 0), (0, LANES - share)))
    lines = [[g for g in range(devices) if g // SIDE == y] for y in range(SIDE)]
    gathered = lax.all_gather(subspace, "gvec", axis_index_groups=lines)

    live = (jnp.arange(slots, dtype=jnp.int32) < counts[0]).astype(jnp.float32)
    live_rows = jnp.repeat(live, states).reshape(devices, rows, 1)
    weight_rows = jnp.repeat(band_weight * live, states).reshape(devices, rows)
    freq_rows = freq_index.reshape(devices, rows)
    order = [(((why - d) & (SIDE - 1)) * SIDE + ex) for d in range(SIDE)]
    freq_here = jnp.concatenate([lax.dynamic_index_in_dim(freq_rows, p, 0, False) for p in order])
    weight_here = jnp.concatenate([lax.dynamic_index_in_dim(weight_rows, p, 0, False) for p in order])
    pick = jnp.where(
        freq_here[None, :] == jnp.arange(nodes, dtype=jnp.int32)[:, None], weight_here[None, :], jnp.float32(0.0)
    )[:, :, None]
    live_here = lax.dynamic_index_in_dim(live_rows, gvec, 0, False)

    full = [(0, 0)]
    halves = [(0, 0), (HALF, 0)]

    def lay(forms):
        return [(row, n * LANES) for n, form in enumerate(forms) for row, _ in form]

    ids = [2 * zed + core, 2 * zed + 1 - core]
    up = down = mine
    codes = []

    def send(pieces, forms):
        code = project(flat, pieces, lay(forms), len(forms) * LANES, devices)
        codes.append(lax.all_to_all(code, "gvec", 0, 0))

    held = [mine, sibling(mine)]
    forms = [full, full]
    for step in range(1, chips // 2 + 1):
        last = step == chips // 2
        up = shift(up[:HALF] if last else up, 1)
        down = shift(down[HALF:] if last else down, -1)
        send(held, forms)
        up_z, down_z = 2 * ((zed - step) & (chips - 1)), 2 * ((zed + step) & (chips - 1))
        if last:
            held = [up, down, sibling(up), sibling(down)]
            forms = [halves, halves]
            ids += [up_z + core, up_z + 1 - core]
        else:
            held = [up, sibling(up), down, sibling(down)]
            forms = [full] * 4
            ids += [up_z + core, up_z + 1 - core, down_z + core, down_z + 1 - core]
    send(held, forms)

    parts = [collect(code, live_here) for code in codes]
    coef = jnp.concatenate([p[0] for p in parts], axis=0)
    rounded = jnp.concatenate([p[1] for p in parts], axis=0)
    around = [rounded] + [along_y(rounded, d) for d in range(1, SIDE)]
    ids = jnp.stack(ids).astype(jnp.int32)
    span = jnp.arange(bands, dtype=jnp.int32)
    place = jnp.sum(jnp.where(ids[None, :] == span[:, None], span[None, :], 0), axis=1)
    own = lax.dynamic_slice_in_dim(place, why * SIDE, SIDE, 0)
    message = quadratic(place, own, gathered, pick, coef, around, share)
    landed = lax.all_to_all(message, "gvec", 0, 0)
    coef_out = landed[:, 0:rows, 0:share].reshape(slots, states, share)
    terms = jnp.sum(landed[:, rows : rows + states, 0], axis=0)
    spread = lax.all_to_all(jnp.broadcast_to(terms, (bands, states)), "band", 0, 0)
    total = jnp.sum(spread, axis=0)
    scale_factor = math.sqrt(NEIG * bands * slots)
    sigma = -total / jnp.float32(scale_factor)
    return (coef_out, sigma)


def solution(mesh):
    in_specs = (
        P("band", None, "gvec"),
        P("gvec", "band"),
        P(None, "gvec", None),
        P("band"),
        P("band", None),
        P("band"),
    )
    out_specs = (P("band", None, "gvec"), P())
    return jax.shard_map(local, mesh=mesh, in_specs=in_specs, out_specs=out_specs, check_vma=False)
```

```python
import math

import jax
import jax.numpy as jnp
from jax import lax
from jax.experimental import pallas as pl
from jax.experimental.pallas import tpu as pltpu
from jax.sharding import PartitionSpec as P

NEIG = 2000
LANES = 128
LIMIT = 32000.0
STEPS = 24
SIDE = 4
CUT = 1920
EARLY = 3
SMALL = 24 * 1024 * 1024
ANYWHERE = pl.BlockSpec(memory_space=pl.ANY)
IN_VMEM = pl.BlockSpec(memory_space=pltpu.VMEM)
IN_SMEM = pl.BlockSpec(memory_space=pltpu.SMEM)


def spread_kernel(w_ref, out_ref):
    nodes, share, _ = w_ref.shape
    blocks = out_ref.shape[2] // LANES
    out_ref[...] = jnp.zeros_like(out_ref)
    for node in range(nodes):
        for k in range(blocks):
            out_ref[node, 0:share, k * LANES : k * LANES + share] = w_ref[node, :, k * share : (k + 1) * share]


def spread(subspace):
    nodes, share, neig = subspace.shape
    return pl.pallas_call(
        spread_kernel,
        in_specs=[IN_VMEM],
        out_specs=IN_VMEM,
        out_shape=jax.ShapeDtypeStruct((nodes, LANES, neig // share * LANES), subspace.dtype),
        compiler_params=pltpu.CompilerParams(vmem_limit_bytes=SMALL),
        name="spread",
    )(subspace)


def project_kernel(count, own_ref, other_ref, *refs):
    out_ref = refs[-1]
    rhs = jnp.concatenate(
        [jnp.concatenate([refs[2 * n][...], refs[2 * n + 1][...]], axis=0) for n in range(count)], axis=1
    )
    cols = count * LANES
    parts, rows = out_ref.shape[:2]
    powers = []
    for side, ref in enumerate((own_ref, other_ref)):
        total = jnp.dot(ref[...], rhs, preferred_element_type=jnp.float32)
        most = jnp.max(jnp.abs(total), axis=1, keepdims=True)
        scale = jnp.ones_like(most)
        power = jnp.zeros(most.shape, jnp.int32)
        for i in range(1, STEPS + 1):
            fits = most * float(2**i) <= LIMIT
            scale = jnp.where(fits, float(2**i), scale)
            power = jnp.where(fits, i, power)
        code = jnp.round(total * scale).astype(jnp.int32).astype(jnp.int16)
        out_ref[:, :, side * cols : (side + 1) * cols] = code.reshape(parts, rows, cols)
        powers.append(jnp.broadcast_to(power, (power.shape[0], LANES)))
    lane = lax.broadcasted_iota(jnp.int32, powers[0].shape, 1)
    wide = jnp.where(lane < LANES // 2, powers[0], powers[1]).astype(jnp.int16)
    out_ref[:, :, 2 * cols : 2 * cols + LANES] = wide.reshape(parts, rows, LANES)


def project(own, other, blocks, devices, ahead=()):
    nrows, depth = own.shape
    count = len(blocks)
    share = nrows // devices
    halves = [half for block in blocks for half in block]
    return pl.pallas_call(
        lambda *refs: project_kernel(count, *refs),
        in_specs=[IN_VMEM] * (2 + len(halves)) + [ANYWHERE] * len(ahead),
        out_specs=IN_VMEM,
        out_shape=jax.ShapeDtypeStruct((devices, share, (2 * count + 1) * LANES), jnp.int16),
        compiler_params=pltpu.CompilerParams(vmem_limit_bytes=SMALL),
        cost_estimate=pl.CostEstimate(
            flops=4 * nrows * depth * count * LANES, bytes_accessed=4 * nrows * depth, transcendentals=0
        ),
        name="project",
    )(own, other, *halves, *ahead)


def collect_kernel(code_ref, mine_ref, other_ref):
    devices, rows, width = code_ref.shape
    cols = (width - LANES) // 2
    totals = [jnp.zeros((rows, cols), jnp.float32) for _ in range(2)]
    for d in range(devices):
        powers = code_ref[d, :, 2 * cols : 2 * cols + LANES].astype(jnp.int32)
        for side in range(2):
            power = powers[:, side * (LANES // 2) : side * (LANES // 2) + 1]
            unit = 1.0 / (jnp.ones_like(power) << power).astype(jnp.float32)
            code = code_ref[d, :, side * cols : (side + 1) * cols].astype(jnp.int32).astype(jnp.float32)
            totals[side] += code * unit
    for n in range(cols // LANES):
        mine_ref[n] = totals[0][:, n * LANES : (n + 1) * LANES]
        other_ref[n] = totals[1][:, n * LANES : (n + 1) * LANES]


def collect(code):
    devices, rows, width = code.shape
    shape = jax.ShapeDtypeStruct(((width - LANES) // 2 // LANES, rows, LANES), jnp.float32)
    return pl.pallas_call(
        collect_kernel,
        in_specs=[IN_VMEM],
        out_specs=(IN_VMEM, IN_VMEM),
        out_shape=(shape, shape),
        compiler_params=pltpu.CompilerParams(vmem_limit_bytes=SMALL),
        name="collect",
    )(code)


def settle_kernel(count, live_ref, *refs):
    pieces, coef_ref, rounded_ref = refs[:count], refs[count], refs[count + 1]
    at = 0
    for piece in pieces:
        for n in range(piece.shape[0]):
            value = piece[n] * live_ref[...]
            coef_ref[at] = value
            rounded_ref[at] = value.astype(jnp.bfloat16)
            at += 1


def settle(live_rows, pieces):
    total = sum(p.shape[0] for p in pieces)
    rows = pieces[0].shape[1]
    return pl.pallas_call(
        lambda *refs: settle_kernel(len(pieces), *refs),
        in_specs=[IN_VMEM] * (1 + len(pieces)),
        out_specs=(IN_VMEM, IN_VMEM),
        out_shape=(
            jax.ShapeDtypeStruct((total, rows, LANES), jnp.float32),
            jax.ShapeDtypeStruct((total, rows, LANES), jnp.bfloat16),
        ),
        compiler_params=pltpu.CompilerParams(vmem_limit_bytes=SMALL),
        name="settle",
    )(live_rows, *pieces)


def quad_kernel(groups, tables, ids_ref, own_ref, node_ref, pick_ref, *refs):
    coefs, refs = refs[:groups], refs[groups:]
    pieces, refs = refs[: groups * SIDE], refs[groups * SIDE :]
    weights, out_ref, flat = refs[:tables], refs[tables], refs[tables + 1]
    rows = coefs[0].shape[1]
    blocks = out_ref.shape[0]
    at = 0
    for g in range(groups):
        for n in range(coefs[g].shape[0]):
            k = ids_ref[at]
            out_ref[k, 0:rows, :] = coefs[g][n]
            lane = pl.ds(pl.multiple_of(k * LANES, LANES), LANES)
            for d in range(SIDE):
                flat[d * rows : (d + 1) * rows, lane] = pieces[g * SIDE + d][n]
            at += 1
    right = flat[...]
    total = jnp.zeros((1, SIDE * rows), jnp.float32)
    for i, ref in enumerate(weights):
        k = own_ref[i]
        left = flat[:, pl.ds(pl.multiple_of(k * LANES, LANES), LANES)].astype(jnp.float32).T
        count = ref.shape[0]
        applied = lax.dot_general(
            ref[...].reshape(count * LANES, ref.shape[2]),
            right,
            (((1,), (1,)), ((), ())),
            preferred_element_type=jnp.float32,
        )
        for n in range(count):
            value = jnp.sum(left * applied[n * LANES : (n + 1) * LANES], axis=0, keepdims=True)
            total += value * pick_ref[pl.ds(node_ref[i] + n, 1), :]
    first = jnp.zeros((8, LANES), jnp.float32)
    line = lax.broadcasted_iota(jnp.int32, (8, LANES), 0)
    rest = jnp.concatenate([total[:, LANES:], jnp.zeros((1, 2 * LANES - SIDE * rows), jnp.float32)], axis=1)
    first = jnp.where(line == 0, total[:, 0:LANES], jnp.where(line == 1, rest, 0.0))
    for k in range(blocks):
        out_ref[k, rows : rows + 8, :] = first


def quadratic(ids, own, nodes_at, pick, coefs, pieces, weights):
    rows = coefs[0].shape[1]
    blocks = sum(c.shape[0] for c in coefs)
    return pl.pallas_call(
        lambda *refs: quad_kernel(len(coefs), len(weights), *refs),
        in_specs=[IN_SMEM] * 3 + [IN_VMEM] * (1 + len(coefs) + len(pieces) + len(weights)),
        out_specs=IN_VMEM,
        out_shape=jax.ShapeDtypeStruct((blocks, rows + 8, LANES), jnp.float32),
        scratch_shapes=[pltpu.VMEM((SIDE * rows, blocks * LANES), jnp.bfloat16)],
        compiler_params=pltpu.CompilerParams(vmem_limit_bytes=SMALL),
        name="quad",
    )(ids, own, nodes_at, pick, *coefs, *pieces, *weights)


def local(pair_density, eigvecs, subspace, counts, freq_index, band_weight):
    slots, states, depth = pair_density.shape
    nodes, share, neig = subspace.shape
    devices = lax.axis_size("gvec")
    bands = lax.axis_size("band")
    chips = bands // 2
    nrows = slots * states
    rows = nrows // devices
    band, gvec = lax.axis_index("band"), lax.axis_index("gvec")
    zed, core = band >> 1, band & 1
    why, ex = gvec >> 2, gvec & 3

    def shift(value, by):
        return lax.ppermute(value, "band", [(b, (b + 2 * by) % bands) for b in range(bands)])

    def sibling(value):
        return lax.ppermute(value, "band", [(b, b ^ 1) for b in range(bands)])

    def along_y(value, by):
        return lax.ppermute(value, "gvec", [(g, (g + SIDE * by) % devices) for g in range(devices)])

    def along_x(value, by):
        return lax.ppermute(value, "gvec", [(g, g // SIDE * SIDE + (g + by) % SIDE) for g in range(devices)])

    flat = pair_density.reshape(nrows, depth)
    other = sibling(flat)
    mine = jnp.pad(eigvecs, ((0, 0), (0, LANES - share)))
    mine = (mine[:CUT], mine[CUT:])

    table = spread(subspace)
    pair = nodes // 2
    sent = lax.dynamic_slice_in_dim(table, core * pair, pair, 0)
    before, after = along_x(sent, 1), along_x(sent, -1)
    across = [along_x(before[: pair // 2], 1), along_x(after[pair // 2 :], -1)]
    remote = [before, after] + across
    weights = [table] + remote + [sibling(w) for w in remote]
    there = 1 - core
    nodes_at = [0] + [c * pair + n for c in (core, there) for n in (0, 0, 0, pair // 2)]
    x_at = [ex] + [(ex + d) & (SIDE - 1) for _ in range(2) for d in (-1, 1, 2, 2)]
    nodes_at = jnp.stack([jnp.int32(n) for n in nodes_at])
    own = jnp.stack([why * SIDE + x for x in x_at]).astype(jnp.int32)

    live = (jnp.arange(slots, dtype=jnp.int32) < counts[0]).astype(jnp.float32)
    live_rows = jnp.repeat(live, states).reshape(devices, rows, 1)
    weight_rows = jnp.repeat(band_weight * live, states).reshape(devices, rows)
    freq_rows = freq_index.reshape(devices, rows)
    order = [(((why - d) & (SIDE - 1)) * SIDE + ex) for d in range(SIDE)]
    freq_here = jnp.concatenate([lax.dynamic_index_in_dim(freq_rows, p, 0, False) for p in order])
    weight_here = jnp.concatenate([lax.dynamic_index_in_dim(weight_rows, p, 0, False) for p in order])
    pick = jnp.where(
        freq_here[None, :] == jnp.arange(nodes, dtype=jnp.int32)[:, None], weight_here[None, :], jnp.float32(0.0)
    )
    live_here = lax.dynamic_index_in_dim(live_rows, gvec, 0, False)

    steps = chips // 2
    places = [[zed]]
    for step in range(1, steps):
        places.append([(zed - step) & (chips - 1), (zed + step) & (chips - 1)])
    places.append([(zed + steps) & (chips - 1)])
    split = [(0, EARLY), (EARLY, steps + 1)]
    ids = []
    for begin, end in split:
        for c in (core, there):
            ids += [2 * z + c for step in range(begin, end) for z in places[step]]
    ids = jnp.stack(ids).astype(jnp.int32)

    def send(blocks, ahead=()):
        return lax.all_to_all(project(flat, other, blocks, devices, ahead), "gvec", 0, 0)

    up = down = mine
    held = [mine]
    codes = []
    for step in range(1, steps + 1):
        if step < steps:
            up = tuple(shift(half, 1) for half in up)
            down = tuple(shift(half, -1) for half in down)
            arrived = [up, down]
        else:
            arrived = [(shift(up[0], 1), shift(down[1], -1))]
        codes.append(send(held, (pick, live_here, ids, own, nodes_at) if step == 1 else ()))
        held = arrived
    codes.append(send(held))

    parts = [collect(code) for code in codes]
    coefs, pieces = [], []
    for begin, end in split:
        swapped = sibling(jnp.concatenate([p[1] for p in parts[begin:end]], axis=0))
        coef, rounded = settle(live_here, [p[0] for p in parts[begin:end]] + [swapped])
        coefs.append(coef)
        pieces += [rounded] + [along_y(rounded, d) for d in range(1, SIDE)]
    message = quadratic(ids, own, nodes_at, pick, coefs, pieces, weights)
    landed = lax.all_to_all(message, "gvec", 0, 0)
    coef_out = landed[:, 0:rows, 0:share].reshape(slots, states, share)
    terms = jnp.sum(landed[:, rows : rows + 2, :], axis=0)
    terms = jnp.sum(terms.reshape(2 * LANES // states, states), axis=0)
    spread_terms = lax.all_to_all(jnp.broadcast_to(terms, (bands, states)), "band", 0, 0)
    total = jnp.sum(spread_terms, axis=0)
    scale_factor = math.sqrt(NEIG * bands * slots)
    sigma = -total / jnp.float32(scale_factor)
    return (coef_out, sigma)


def solution(mesh):
    in_specs = (
        P("band", None, "gvec"),
        P("gvec", "band"),
        P(None, "gvec", None),
        P("band"),
        P("band", None),
        P("band"),
    )
    out_specs = (P("band", None, "gvec"), P())
    return jax.shard_map(local, mesh=mesh, in_specs=in_specs, out_specs=out_specs, check_vma=False)
```

```python
import math

import jax
import jax.numpy as jnp
from jax import lax
from jax.experimental import pallas as pl
from jax.experimental.pallas import tpu as pltpu
from jax.sharding import PartitionSpec as P

NEIG = 2000
LANES = 128
LIMIT = 32000.0
STEPS = 24
SIDE = 4
GROUPS = ((0, 2), (2, 3), (3, 5))
SPLIT = 2
MEGA = 1024 * 1024
ANYWHERE = pl.BlockSpec(memory_space=pl.ANY)
IN_VMEM = pl.BlockSpec(memory_space=pltpu.VMEM)
IN_HBM = pl.BlockSpec(memory_space=pltpu.HBM)
IN_SMEM = pl.BlockSpec(memory_space=pltpu.SMEM)


def pin(value):
    return pltpu.with_memory_space_constraint(value, pltpu.HBM)


def spread_kernel(w_ref, out_ref):
    nodes, share, _ = w_ref.shape
    blocks = out_ref.shape[2] // LANES
    out_ref[...] = jnp.zeros_like(out_ref)
    for node in range(nodes):
        for k in range(blocks):
            out_ref[node, 0:share, k * LANES : k * LANES + share] = w_ref[node, :, k * share : (k + 1) * share]


def spread(subspace):
    nodes, share, neig = subspace.shape
    return pl.pallas_call(
        spread_kernel,
        in_specs=[IN_VMEM],
        out_specs=IN_VMEM,
        out_shape=jax.ShapeDtypeStruct((nodes, LANES, neig // share * LANES), subspace.dtype),
        compiler_params=pltpu.CompilerParams(vmem_limit_bytes=16 * MEGA),
        name="spread",
    )(subspace)


def project_kernel(shape, pd_ref, *refs):
    out_ref = refs[-1]
    at, columns = 0, []
    for count in shape:
        parts = [ref[...] for ref in refs[at : at + count]]
        columns.append(parts[0] if count == 1 else jnp.concatenate(parts, axis=0))
        at += count
    total = jnp.dot(pd_ref[...], jnp.concatenate(columns, axis=1), preferred_element_type=jnp.float32)
    most = jnp.max(jnp.abs(total), axis=1, keepdims=True)
    scale = jnp.ones_like(most)
    power = jnp.zeros(most.shape, jnp.int32)
    for j in range(1, STEPS + 1):
        fits = most * float(2**j) <= LIMIT
        scale = jnp.where(fits, float(2**j), scale)
        power = jnp.where(fits, j, power)
    code = jnp.round(total * scale).astype(jnp.int32).astype(jnp.int16)
    devices, rows, width = out_ref.shape
    cols = width - LANES
    out_ref[:, :, 0:cols] = code.reshape(devices, rows, cols)
    wide = jnp.broadcast_to(power, (power.shape[0], LANES)).astype(jnp.int16)
    out_ref[:, :, cols:width] = wide.reshape(devices, rows, LANES)


def project(flat, blocks, devices, ahead=()):
    nrows, depth = flat.shape
    share = nrows // devices
    shape = [len(block) for block in blocks]
    parts = [part for block in blocks for part in block]
    width = (len(blocks) + 1) * LANES
    return pl.pallas_call(
        lambda pd_ref, *refs: project_kernel(shape, pd_ref, *refs[: len(parts)], refs[-1]),
        grid=(SPLIT,),
        in_specs=[pl.BlockSpec((nrows // SPLIT, depth), lambda i: (i, 0))]
        + [pl.BlockSpec(part.shape, lambda i: (0, 0)) for part in parts]
        + [ANYWHERE] * len(ahead),
        out_specs=pl.BlockSpec((devices // SPLIT, share, width), lambda i: (i, 0, 0)),
        out_shape=pltpu.HBM((devices, share, width), jnp.int16),
        compiler_params=pltpu.CompilerParams(vmem_limit_bytes=32 * MEGA),
        cost_estimate=pl.CostEstimate(flops=10**6, bytes_accessed=10**4, transcendentals=0),
        name="project",
    )(pin(flat), *parts, *ahead)


def collect_kernel(count, live_ref, *refs):
    codes, coef_ref, rounded_ref = refs[:count], refs[count], refs[count + 1]
    at = 0
    for code_ref in codes:
        devices, rows, width = code_ref.shape
        cols = width - LANES
        total = jnp.zeros((rows, cols), jnp.float32)
        for d in range(devices):
            power = code_ref[d, :, cols : cols + LANES].astype(jnp.int32)[:, 0:1]
            unit = 1.0 / (jnp.ones_like(power) << power).astype(jnp.float32)
            total += code_ref[d, :, 0:cols].astype(jnp.int32).astype(jnp.float32) * unit
        total = total * live_ref[...]
        for n in range(cols // LANES):
            part = total[:, n * LANES : (n + 1) * LANES]
            coef_ref[at] = part
            rounded_ref[at] = part.astype(jnp.bfloat16)
            at += 1


def collect(codes, live_rows, ahead=()):
    rows = codes[0].shape[1]
    total = sum(code.shape[2] // LANES - 1 for code in codes)
    return pl.pallas_call(
        lambda *refs: collect_kernel(len(codes), *refs[: 1 + len(codes)], *refs[-2:]),
        in_specs=[IN_VMEM] * (1 + len(codes)) + [ANYWHERE] * len(ahead),
        out_specs=(IN_VMEM, IN_VMEM),
        out_shape=(
            jax.ShapeDtypeStruct((total, rows, LANES), jnp.float32),
            jax.ShapeDtypeStruct((total, rows, LANES), jnp.bfloat16),
        ),
        compiler_params=pltpu.CompilerParams(vmem_limit_bytes=12 * MEGA),
        name="collect",
    )(live_rows, *codes, *ahead)


def quad_kernel(groups, tables, ids_ref, own_ref, node_ref, pick_ref, *refs):
    coefs, refs = refs[:groups], refs[groups:]
    pieces, refs = refs[: groups * SIDE], refs[groups * SIDE :]
    weights, (out_ref, flat, store, sems) = refs[:tables], refs[tables:]
    rows = coefs[0].shape[1]
    blocks = out_ref.shape[0]
    copies, at = [], 0
    for i, ref in enumerate(weights):
        copies.append(pltpu.make_async_copy(ref, store.at[at : at + ref.shape[0]], sems.at[i]))
        copies[-1].start()
        at += ref.shape[0]
    at = 0
    for g in range(groups):
        for n in range(coefs[g].shape[0]):
            k = ids_ref[at]
            out_ref[k, 0:rows, :] = coefs[g][n]
            lane = pl.ds(pl.multiple_of(k * LANES, LANES), LANES)
            for d in range(SIDE):
                flat[d * rows : (d + 1) * rows, lane] = pieces[g * SIDE + d][n]
            at += 1
    right = flat[...]
    total = jnp.zeros((1, SIDE * rows), jnp.float32)
    base = 0
    for i, ref in enumerate(weights):
        copies[i].wait()
        k = own_ref[i]
        left = flat[:, pl.ds(pl.multiple_of(k * LANES, LANES), LANES)].astype(jnp.float32).T
        count = ref.shape[0]
        applied = lax.dot_general(
            store[base : base + count].reshape(count * LANES, ref.shape[2]),
            right,
            (((1,), (1,)), ((), ())),
            preferred_element_type=jnp.float32,
        )
        for n in range(count):
            value = jnp.sum(left * applied[n * LANES : (n + 1) * LANES], axis=0, keepdims=True)
            total += value * pick_ref[pl.ds(node_ref[i] + n, 1), :]
        base += count
    first = jnp.zeros((8, LANES), jnp.float32)
    line = lax.broadcasted_iota(jnp.int32, (8, LANES), 0)
    rest = jnp.concatenate([total[:, LANES:], jnp.zeros((1, 2 * LANES - SIDE * rows), jnp.float32)], axis=1)
    first = jnp.where(line == 0, total[:, 0:LANES], jnp.where(line == 1, rest, 0.0))
    for k in range(blocks):
        out_ref[k, rows : rows + 8, :] = first


def quadratic(ids, own, nodes_at, pick, coefs, pieces, weights):
    rows = coefs[0].shape[1]
    blocks = sum(c.shape[0] for c in coefs)
    return pl.pallas_call(
        lambda *refs: quad_kernel(len(coefs), len(weights), *refs),
        in_specs=[IN_SMEM] * 3 + [IN_VMEM] * (1 + len(coefs) + len(pieces)) + [IN_HBM] * len(weights),
        out_specs=IN_VMEM,
        out_shape=jax.ShapeDtypeStruct((blocks, rows + 8, LANES), jnp.float32),
        scratch_shapes=[
            pltpu.VMEM((SIDE * rows, blocks * LANES), jnp.bfloat16),
            pltpu.VMEM((sum(w.shape[0] for w in weights), LANES, blocks * LANES), jnp.bfloat16),
            pltpu.SemaphoreType.DMA((len(weights),)),
        ],
        compiler_params=pltpu.CompilerParams(vmem_limit_bytes=20 * MEGA),
        name="quad",
    )(ids, own, nodes_at, pick, *coefs, *pieces, *map(pin, weights))


def local(pair_density, eigvecs, subspace, counts, freq_index, band_weight):
    slots, states, depth = pair_density.shape
    nodes, share, neig = subspace.shape
    devices = lax.axis_size("gvec")
    bands = lax.axis_size("band")
    chips = bands // 2
    nrows = slots * states
    rows = nrows // devices
    band, gvec = lax.axis_index("band"), lax.axis_index("gvec")
    zed, core = band >> 1, band & 1
    why, ex = gvec >> 2, gvec & 3

    def shift(value, by):
        return lax.ppermute(value, "band", [(b, (b + 2 * by) % bands) for b in range(bands)])

    def sibling(value):
        return lax.ppermute(value, "band", [(b, b ^ 1) for b in range(bands)])

    def along_y(value, by):
        return lax.ppermute(value, "gvec", [(g, (g + SIDE * by) % devices) for g in range(devices)])

    def along_x(value):
        pairs = []
        for b in range(bands):
            for g in range(devices):
                to = g // SIDE * SIDE + (g + (1 if b % 2 == 0 else -1)) % SIDE
                pairs.append((b * devices + g, b * devices + to))
        return lax.ppermute(value, ("band", "gvec"), pairs)

    def along_z(value):
        return lax.ppermute(value, "band", [(b, (b + (2 if b % 2 == 0 else -2)) % bands) for b in range(bands)])

    flat = pair_density.reshape(nrows, depth)
    there, pair = 1 - core, nodes // 2
    turn = 2 * core - 1
    nodes_at = jnp.stack([0 * core, 0 * core, 0 * core, core * pair, there * pair]).astype(jnp.int32)
    x_at = [ex + d for d in (0, turn, -turn, 2, 2)]
    own = jnp.stack([why * SIDE + (x & (SIDE - 1)) for x in x_at]).astype(jnp.int32)

    steps = chips // 2
    places = [[zed]]
    for step in range(1, steps):
        places.append([(zed - step) & (chips - 1), (zed + step) & (chips - 1)])
    places.append([(zed + steps) & (chips - 1)])
    ids = []
    for begin, end in GROUPS:
        ids += [2 * z + c for step in range(begin, end) for z in places[step] for c in (core, there)]
    ids = jnp.stack(ids).astype(jnp.int32)


    def window(run, *operands):
        like = jax.eval_shape(run, *operands)
        return lax.cond(
            counts[0] > 0, run, lambda *_: jax.tree.map(lambda v: jnp.zeros(v.shape, v.dtype), like), *operands
        )

    def spread_rows(rounded):
        return [rounded] + [along_y(rounded, d) for d in range(1, SIDE)]

    def pair_up(blocks):
        return [part for block in blocks for part in (block, tuple(sibling(half) for half in block))]

    def send(code):
        return lax.all_to_all(code, "gvec", 0, 0)

    def first(flat, eigvecs, subspace, band_weight, freq_index):
        mine = jnp.pad(eigvecs, ((0, 0), (0, LANES - share)))
        up, down = shift(mine, 1), shift(mine, -1)
        table = spread(subspace)
        near = along_x(table)
        code = project(flat, pair_up([(mine,)]), devices)
        live = (jnp.arange(slots, dtype=jnp.int32) < counts[0]).astype(jnp.float32)
        live_rows = jnp.repeat(live, states).reshape(devices, rows, 1)
        weight_rows = jnp.repeat(band_weight * live, states).reshape(devices, rows)
        freq_rows = freq_index.reshape(devices, rows)
        order = [(((why - d) & (SIDE - 1)) * SIDE + ex) for d in range(SIDE)]
        freq_here = jnp.concatenate([lax.dynamic_index_in_dim(freq_rows, p, 0, False) for p in order])
        weight_here = jnp.concatenate([lax.dynamic_index_in_dim(weight_rows, p, 0, False) for p in order])
        pick = jnp.where(
            freq_here[None, :] == jnp.arange(nodes, dtype=jnp.int32)[:, None], weight_here[None, :], jnp.float32(0.0)
        )
        live_here = lax.dynamic_index_in_dim(live_rows, gvec, 0, False)

        return up, down, code, table, near, pick, live_here

    def second(flat, up, down, code):
        code_now = project(flat, pair_up([(up,), (down,)]), devices)
        return shift(up, 1), shift(down, -1), code_now, send(code)

    def third(flat, up, down, code, near):
        code_now = project(flat, pair_up([(up,), (down,)]), devices)
        across = along_x(lax.dynamic_slice_in_dim(near, core * pair, pair, 0))
        return shift(up, 1), shift(down, -1), code_now, send(code), across

    def fourth(up, down, code, landing, live_here):
        far = along_z(jnp.where(core == 0, up, down))
        coef, rounded = collect(landing, live_here)
        return [far, sibling(up), sibling(down)], send(code), coef, spread_rows(rounded)

    def fifth(flat, up, down, arrived, landing, live_here, near, across):
        far, up_beside, down_beside = arrived
        blocks = [(b,) for b in (up, up_beside, down, down_beside, far, sibling(far))]
        code = project(flat, blocks, devices)
        coef, rounded = collect(landing, live_here)
        return send(code), coef, spread_rows(rounded), sibling(near), sibling(across)

    def sixth(landing, live_here):
        coef, rounded = collect(landing, live_here)
        return coef, spread_rows(rounded)

    up, down, code, table, near, pick, live_here = window(first, flat, eigvecs, subspace, band_weight, freq_index)
    up, down, code, landed_0 = window(second, flat, up, down, code)
    up, down, code, landed_1, across = window(third, flat, up, down, code, near)
    arrived, landed_2, coef_a, pieces_a = window(fourth, up, down, code, [landed_0, landed_1], live_here)
    landed_3, coef_b, pieces_b, near_swapped, across_swapped = window(
        fifth, flat, up, down, arrived, [landed_2], live_here, near, across
    )
    coef_c, pieces_c = window(sixth, [landed_3], live_here)
    weights = [table, near, near_swapped, across, across_swapped]
    coefs, pieces = [coef_a, coef_b, coef_c], pieces_a + pieces_b + pieces_c
    message = quadratic(ids, own, nodes_at, pick, coefs, pieces, weights)
    landed = lax.all_to_all(message, "gvec", 0, 0)
    coef_out = landed[:, 0:rows, 0:share].reshape(slots, states, share)
    terms = jnp.sum(landed[:, rows : rows + 2, :], axis=0)
    terms = jnp.sum(terms.reshape(2 * LANES // states, states), axis=0)
    spread_terms = lax.all_to_all(jnp.broadcast_to(terms, (bands, states)), "band", 0, 0)
    total = jnp.sum(spread_terms, axis=0)
    scale_factor = math.sqrt(NEIG * bands * slots)
    sigma = -total / jnp.float32(scale_factor)
    return (coef_out, sigma)


def solution(mesh):
    in_specs = (
        P("band", None, "gvec"),
        P("gvec", "band"),
        P(None, "gvec", None),
        P("band"),
        P("band", None),
        P("band"),
    )
    out_specs = (P("band", None, "gvec"), P())
    return jax.shard_map(local, mesh=mesh, in_specs=in_specs, out_specs=out_specs, check_vma=False)
```

```python
import math

import jax
import jax.numpy as jnp
from jax import lax
from jax.experimental import pallas as pl
from jax.experimental.pallas import tpu as pltpu
from jax.sharding import PartitionSpec as P

NEIG = 2000
LANES = 128
LIMIT = 32000.0
STEPS = 24
SIDE = 4
GROUPS = ((0, 2), (2, 5))
SPLIT = 4
MEGA = 1024 * 1024
ANYWHERE = pl.BlockSpec(memory_space=pl.ANY)
IN_VMEM = pl.BlockSpec(memory_space=pltpu.VMEM)
IN_HBM = pl.BlockSpec(memory_space=pltpu.HBM)
IN_SMEM = pl.BlockSpec(memory_space=pltpu.SMEM)


def pin(value):
    return pltpu.with_memory_space_constraint(value, pltpu.HBM)


def spread_kernel(first_ref, w_ref, *outs):
    share = w_ref.shape[1]
    for side, ref in enumerate(outs):
        count, _, width = ref.shape
        ref[...] = jnp.zeros_like(ref)

        def one(n, carry, side=side, ref=ref):
            rows = w_ref[first_ref[side] + n]
            for k in range(width // LANES):
                ref[n, 0:share, k * LANES : k * LANES + share] = rows[:, k * share : (k + 1) * share]
            return carry

        lax.fori_loop(0, count, one, 0)


def spread(first, subspace):
    nodes, share, neig = subspace.shape
    half = jax.ShapeDtypeStruct((nodes // 2, LANES, neig // share * LANES), subspace.dtype)
    return pl.pallas_call(
        spread_kernel,
        in_specs=[IN_SMEM, IN_VMEM],
        out_specs=[IN_VMEM, IN_VMEM],
        out_shape=[half, half],
        compiler_params=pltpu.CompilerParams(vmem_limit_bytes=16 * MEGA),
        name="spread",
    )(first, subspace)


def project_kernel(shape, pd_ref, *refs):
    out_ref = refs[-1]
    at, columns = 0, []
    for count in shape:
        parts = [ref[...] for ref in refs[at : at + count]]
        columns.append(parts[0] if count == 1 else jnp.concatenate(parts, axis=0))
        at += count
    total = jnp.dot(pd_ref[...], jnp.concatenate(columns, axis=1), preferred_element_type=jnp.float32)
    most = jnp.max(jnp.abs(total), axis=1, keepdims=True)
    scale = jnp.ones_like(most)
    power = jnp.zeros(most.shape, jnp.int32)
    for j in range(1, STEPS + 1):
        fits = most * float(2**j) <= LIMIT
        scale = jnp.where(fits, float(2**j), scale)
        power = jnp.where(fits, j, power)
    code = jnp.round(total * scale).astype(jnp.int32)
    lane = lax.broadcasted_iota(jnp.int32, code.shape, 1)
    code = jnp.where(lane == LANES - 1, power, code).astype(jnp.int16)
    out_ref[...] = code.reshape(out_ref.shape)


def project(flat, blocks, devices, ahead=()):
    nrows, depth = flat.shape
    share = nrows // devices
    shape = [len(block) for block in blocks]
    parts = [part for block in blocks for part in block]
    width = len(blocks) * LANES
    return pl.pallas_call(
        lambda pd_ref, *refs: project_kernel(shape, pd_ref, *refs[: len(parts)], refs[-1]),
        grid=(SPLIT,),
        in_specs=[pl.BlockSpec((nrows // SPLIT, depth), lambda i: (i, 0))]
        + [pl.BlockSpec(part.shape, lambda i: (0, 0)) for part in parts]
        + [ANYWHERE] * len(ahead),
        out_specs=pl.BlockSpec((devices // SPLIT, share, width), lambda i: (i, 0, 0)),
        out_shape=pltpu.HBM((devices, share, width), jnp.int16),
        compiler_params=pltpu.CompilerParams(vmem_limit_bytes=32 * MEGA),
        cost_estimate=pl.CostEstimate(flops=10**6, bytes_accessed=10**4, transcendentals=0),
        name="project",
    )(pin(flat), *parts, *ahead)


def collect_kernel(count, live_ref, *refs):
    codes, coef_ref, rounded_ref = refs[:count], refs[count], refs[count + 1]
    at = 0
    for code_ref in codes:
        devices, rows, width = code_ref.shape
        total = jnp.zeros((rows, width), jnp.float32)
        for d in range(devices):
            power = code_ref[d, :, 0:LANES].astype(jnp.int32)[:, LANES - 1 : LANES]
            unit = 1.0 / (jnp.ones_like(power) << power).astype(jnp.float32)
            total += code_ref[d].astype(jnp.int32).astype(jnp.float32) * unit
        lane = lax.broadcasted_iota(jnp.int32, total.shape, 1)
        total = jnp.where(lane == LANES - 1, 0.0, total) * live_ref[...]
        for n in range(width // LANES):
            part = total[:, n * LANES : (n + 1) * LANES]
            coef_ref[at] = part
            rounded_ref[at] = part.astype(jnp.bfloat16)
            at += 1


def collect(codes, live_rows, ahead=()):
    rows = codes[0].shape[1]
    total = sum(code.shape[2] // LANES for code in codes)
    return pl.pallas_call(
        lambda *refs: collect_kernel(len(codes), *refs[: 1 + len(codes)], *refs[-2:]),
        in_specs=[IN_VMEM] * (1 + len(codes)) + [ANYWHERE] * len(ahead),
        out_specs=(IN_VMEM, IN_VMEM),
        out_shape=(
            jax.ShapeDtypeStruct((total, rows, LANES), jnp.float32),
            jax.ShapeDtypeStruct((total, rows, LANES), jnp.bfloat16),
        ),
        compiler_params=pltpu.CompilerParams(vmem_limit_bytes=12 * MEGA),
        name="collect",
    )(live_rows, *codes, *ahead)


def quad_kernel(groups, tables, ids_ref, own_ref, node_ref, pick_ref, *refs):
    coefs, refs = refs[:groups], refs[groups:]
    pieces, refs = refs[: groups * SIDE], refs[groups * SIDE :]
    weights, (out_ref, flat, store, sems) = refs[:tables], refs[tables:]
    rows = coefs[0].shape[1]
    blocks = out_ref.shape[0]
    for i, ref in enumerate(weights):
        count = ref.shape[0]
        pltpu.make_async_copy(ref, store.at[i * count : (i + 1) * count], sems.at[i]).start()
    at = 0
    for g in range(groups):
        for n in range(coefs[g].shape[0]):
            k = ids_ref[at]
            out_ref[k, 0:rows, :] = coefs[g][n]
            lane = pl.ds(pl.multiple_of(k * LANES, LANES), LANES)
            for d in range(SIDE):
                flat[d * rows : (d + 1) * rows, lane] = pieces[g * SIDE + d][n]
            at += 1
    right = flat[...]
    count = weights[0].shape[0]

    def add(i, total):
        pltpu.make_async_copy(store.at[0:count], store.at[pl.ds(i * count, count)], sems.at[i]).wait()
        lane = pl.ds(pl.multiple_of(own_ref[i] * LANES, LANES), LANES)
        left = flat[:, lane].astype(jnp.float32).T
        applied = lax.dot_general(
            store[pl.ds(i * count, count)].reshape(count * LANES, store.shape[2]),
            right,
            (((1,), (1,)), ((), ())),
            preferred_element_type=jnp.float32,
        )
        for n in range(count):
            value = jnp.sum(left * applied[n * LANES : (n + 1) * LANES], axis=0, keepdims=True)
            total += value * pick_ref[pl.ds(node_ref[i] + n, 1), :]
        return total

    total = lax.fori_loop(0, tables, add, jnp.zeros((1, SIDE * rows), jnp.float32))
    first = jnp.zeros((8, LANES), jnp.float32)
    line = lax.broadcasted_iota(jnp.int32, (8, LANES), 0)
    rest = jnp.concatenate([total[:, LANES:], jnp.zeros((1, 2 * LANES - SIDE * rows), jnp.float32)], axis=1)
    first = jnp.where(line == 0, total[:, 0:LANES], jnp.where(line == 1, rest, 0.0))
    for k in range(blocks):
        out_ref[k, rows : rows + 8, :] = first


def quadratic(ids, own, nodes_at, pick, coefs, pieces, weights):
    rows = coefs[0].shape[1]
    blocks = sum(c.shape[0] for c in coefs)
    return pl.pallas_call(
        lambda *refs: quad_kernel(len(coefs), len(weights), *refs),
        in_specs=[IN_SMEM] * 3 + [IN_VMEM] * (1 + len(coefs) + len(pieces)) + [IN_HBM] * len(weights),
        out_specs=IN_VMEM,
        out_shape=jax.ShapeDtypeStruct((blocks, rows + 8, LANES), jnp.float32),
        scratch_shapes=[
            pltpu.VMEM((SIDE * rows, blocks * LANES), jnp.bfloat16),
            pltpu.VMEM((sum(w.shape[0] for w in weights), LANES, blocks * LANES), jnp.bfloat16),
            pltpu.SemaphoreType.DMA((len(weights),)),
        ],
        compiler_params=pltpu.CompilerParams(vmem_limit_bytes=20 * MEGA),
        name="quad",
    )(ids, own, nodes_at, pick, *coefs, *pieces, *map(pin, weights))


def local(pair_density, eigvecs, subspace, counts, freq_index, band_weight):
    slots, states, depth = pair_density.shape
    nodes, share, neig = subspace.shape
    devices = lax.axis_size("gvec")
    bands = lax.axis_size("band")
    chips = bands // 2
    nrows = slots * states
    rows = nrows // devices
    band, gvec = lax.axis_index("band"), lax.axis_index("gvec")
    zed, core = band >> 1, band & 1
    why, ex = gvec >> 2, gvec & 3

    def shift(value, by):
        return lax.ppermute(value, "band", [(b, (b + 2 * by) % bands) for b in range(bands)])

    def sibling(value):
        return lax.ppermute(value, "band", [(b, b ^ 1) for b in range(bands)])

    def along_y(value, by):
        return lax.ppermute(value, "gvec", [(g, (g + SIDE * by) % devices) for g in range(devices)])

    def along_x(value):
        pairs = []
        for b in range(bands):
            for g in range(devices):
                to = g // SIDE * SIDE + (g + (1 if b % 2 == 0 else -1)) % SIDE
                pairs.append((b * devices + g, b * devices + to))
        return lax.ppermute(value, ("band", "gvec"), pairs)

    def along_z(value):
        return lax.ppermute(value, "band", [(b, (b + (2 if b % 2 == 0 else -2)) % bands) for b in range(bands)])

    flat = pair_density.reshape(nrows, depth)
    there, pair = 1 - core, nodes // 2
    turn = 2 * core - 1
    here, beside = core * pair, there * pair
    first_node = jnp.stack([here, beside]).astype(jnp.int32)
    nodes_at = jnp.stack([here, beside, here, beside, beside, here, here, beside]).astype(jnp.int32)
    x_at = [ex + d for d in (0, 0, turn, turn, -turn, -turn, 2, 2)]
    own = jnp.stack([why * SIDE + (x & (SIDE - 1)) for x in x_at]).astype(jnp.int32)

    steps = chips // 2
    places = [[zed]]
    for step in range(1, steps):
        places.append([(zed - step) & (chips - 1), (zed + step) & (chips - 1)])
    places.append([(zed + steps) & (chips - 1)])
    ids = []
    for begin, end in GROUPS:
        ids += [2 * z + c for step in range(begin, end) for z in places[step] for c in (core, there)]
    ids = jnp.stack(ids).astype(jnp.int32)


    def window(run, *operands):
        like = jax.eval_shape(run, *operands)
        return lax.cond(
            counts[0] > 0, run, lambda *_: jax.tree.map(lambda v: jnp.zeros(v.shape, v.dtype), like), *operands
        )

    def spread_rows(rounded):
        return [rounded] + [along_y(rounded, d) for d in range(1, SIDE)]

    def pair_up(blocks):
        return [part for block in blocks for part in (block, tuple(sibling(half) for half in block))]

    def send(code):
        return lax.all_to_all(code, "gvec", 0, 0)

    def first(flat, eigvecs, subspace, band_weight, freq_index):
        mine = jnp.pad(eigvecs, ((0, 0), (0, LANES - share)))
        up, down = shift(mine, 1), shift(mine, -1)
        table = spread(first_node, subspace)
        near = along_x(table[0])
        code = project(flat, pair_up([(mine,)]), devices)
        live = (jnp.arange(slots, dtype=jnp.int32) < counts[0]).astype(jnp.float32)
        live_rows = jnp.repeat(live, states).reshape(devices, rows, 1)
        weight_rows = jnp.repeat(band_weight * live, states).reshape(devices, rows)
        freq_rows = freq_index.reshape(devices, rows)
        order = [(((why - d) & (SIDE - 1)) * SIDE + ex) for d in range(SIDE)]
        freq_here = jnp.concatenate([lax.dynamic_index_in_dim(freq_rows, p, 0, False) for p in order])
        weight_here = jnp.concatenate([lax.dynamic_index_in_dim(weight_rows, p, 0, False) for p in order])
        pick = jnp.where(
            freq_here[None, :] == jnp.arange(nodes, dtype=jnp.int32)[:, None], weight_here[None, :], jnp.float32(0.0)
        )
        live_here = lax.dynamic_index_in_dim(live_rows, gvec, 0, False)

        return up, down, code, table, near, pick, live_here

    def middle(flat, up, down, code, rows_out):
        code_now = project(flat, pair_up([(up,), (down,)]), devices)
        return shift(up, 1), shift(down, -1), code_now, send(code), along_x(rows_out)

    def fourth(flat, up, down, code, landing, live_here):
        far = along_z(jnp.where(core == 0, up, down))
        coef, rounded = collect(landing, live_here)
        return far, project(flat, pair_up([(up,), (down,)]), devices), send(code), coef, rounded

    def fifth(flat, far, code, rounded, near, farther):
        swapped = [sibling(near), sibling(farther)]
        return send(project(flat, pair_up([(far,)]), devices)), send(code), spread_rows(rounded), swapped

    def sixth(landing, live_here, across):
        coef, rounded = collect(landing, live_here)
        return coef, spread_rows(rounded), sibling(across)

    up, down, code, table, near, pick, live_here = window(first, flat, eigvecs, subspace, band_weight, freq_index)
    up, down, code, landed_0, across = window(middle, flat, up, down, code, near)
    up, down, code, landed_1, farther = window(middle, flat, up, down, code, table[1])
    far, code, landed_2, coef_a, rounded = window(fourth, flat, up, down, code, [landed_0, landed_1], live_here)
    landed_4, landed_3, pieces_a, swapped = window(fifth, flat, far, code, rounded, near, farther)
    coef_b, pieces_b, across_swapped = window(sixth, [landed_2, landed_3, landed_4], live_here, across)
    weights = [*table, near, farther, *swapped, across, across_swapped]
    coefs, pieces = [coef_a, coef_b], pieces_a + pieces_b
    message = quadratic(ids, own, nodes_at, pick, coefs, pieces, weights)
    landed = lax.all_to_all(message, "gvec", 0, 0)
    coef_out = landed[:, 0:rows, 0:share].reshape(slots, states, share)
    terms = jnp.sum(landed[:, rows : rows + 2, :], axis=0)
    terms = jnp.sum(terms.reshape(2 * LANES // states, states), axis=0)
    spread_terms = lax.all_to_all(jnp.broadcast_to(terms, (bands, states)), "band", 0, 0)
    total = jnp.sum(spread_terms, axis=0)
    scale_factor = math.sqrt(NEIG * bands * slots)
    sigma = -total / jnp.float32(scale_factor)
    return (coef_out, sigma)


def solution(mesh):
    in_specs = (
        P("band", None, "gvec"),
        P("gvec", "band"),
        P(None, "gvec", None),
        P("band"),
        P("band", None),
        P("band"),
    )
    out_specs = (P("band", None, "gvec"), P())
    return jax.shard_map(local, mesh=mesh, in_specs=in_specs, out_specs=out_specs, check_vma=False)
```

```python
import math

import jax
import jax.numpy as jnp
from jax import lax
from jax.experimental import pallas as pl
from jax.experimental.pallas import tpu as pltpu
from jax.sharding import PartitionSpec as P

NEIG = 2000
LANES = 128
LIMIT = 32000.0
STEPS = 24
SIDE = 4
GROUPS = ((0, 2), (2, 5))
SPLIT = 4
MEGA = 1024 * 1024
ANYWHERE = pl.BlockSpec(memory_space=pl.ANY)
IN_VMEM = pl.BlockSpec(memory_space=pltpu.VMEM)
IN_HBM = pl.BlockSpec(memory_space=pltpu.HBM)
IN_SMEM = pl.BlockSpec(memory_space=pltpu.SMEM)


def pin(value):
    return pltpu.with_memory_space_constraint(value, pltpu.HBM)


def spread_kernel(first_ref, w_ref, *outs):
    share = w_ref.shape[1]
    for side, ref in enumerate(outs):
        count, _, width = ref.shape
        ref[...] = jnp.zeros_like(ref)

        def one(n, carry, side=side, ref=ref):
            rows = w_ref[first_ref[side] + n]
            for k in range(width // LANES):
                ref[n, 0:share, k * LANES : k * LANES + share] = rows[:, k * share : (k + 1) * share]
            return carry

        lax.fori_loop(0, count, one, 0)


def spread(first, subspace):
    nodes, share, neig = subspace.shape
    half = jax.ShapeDtypeStruct((nodes // 2, LANES, neig // share * LANES), subspace.dtype)
    return pl.pallas_call(
        spread_kernel,
        in_specs=[IN_SMEM, IN_VMEM],
        out_specs=[IN_VMEM, IN_VMEM],
        out_shape=[half, half],
        compiler_params=pltpu.CompilerParams(vmem_limit_bytes=16 * MEGA),
        name="spread",
    )(first, subspace)


def project_kernel(shape, pd_ref, *refs):
    out_ref = refs[-1]
    at, columns = 0, []
    for count in shape:
        parts = [ref[...] for ref in refs[at : at + count]]
        columns.append(parts[0] if count == 1 else jnp.concatenate(parts, axis=0))
        at += count
    total = jnp.dot(pd_ref[...], jnp.concatenate(columns, axis=1), preferred_element_type=jnp.float32)
    most = jnp.max(jnp.abs(total), axis=1, keepdims=True)
    scale = jnp.ones_like(most)
    power = jnp.zeros(most.shape, jnp.int32)
    for j in range(1, STEPS + 1):
        fits = most * float(2**j) <= LIMIT
        scale = jnp.where(fits, float(2**j), scale)
        power = jnp.where(fits, j, power)
    code = jnp.round(total * scale).astype(jnp.int32)
    lane = lax.broadcasted_iota(jnp.int32, code.shape, 1)
    code = jnp.where(lane == LANES - 1, power, code).astype(jnp.int16)
    out_ref[...] = code.reshape(out_ref.shape)


def project(flat, blocks, devices, room=0, into=None):
    nrows, depth = flat.shape
    share = nrows // devices
    shape = [len(block) for block in blocks]
    parts = [part for block in blocks for part in block]
    width = len(blocks) * LANES
    whole = width + room * LANES if into is None else into.shape[2]
    place = 0 if into is None else whole // width - 1
    extra = () if into is None else (into,)
    return pl.pallas_call(
        lambda pd_ref, *refs: project_kernel(shape, pd_ref, *refs[: len(parts)], refs[-1]),
        grid=(SPLIT,),
        in_specs=[pl.BlockSpec((nrows // SPLIT, depth), lambda i: (i, 0))]
        + [pl.BlockSpec(part.shape, lambda i: (0, 0)) for part in parts]
        + [ANYWHERE] * len(extra),
        out_specs=pl.BlockSpec((devices // SPLIT, share, width), lambda i: (i, 0, place)),
        out_shape=pltpu.HBM((devices, share, whole), jnp.int16),
        input_output_aliases={1 + len(parts): 0} if extra else {},
        compiler_params=pltpu.CompilerParams(vmem_limit_bytes=32 * MEGA),
        cost_estimate=pl.CostEstimate(flops=10**6, bytes_accessed=10**4, transcendentals=0),
        name="project",
    )(pin(flat), *parts, *map(pin, extra))


def collect_kernel(cuts, kept, live_ref, *refs):
    codes, before, coef_ref, rounded_ref = refs[: len(cuts)], refs[len(cuts) : -2], refs[-2], refs[-1]
    at = kept
    if kept:
        coef_ref[0:kept] = before[0][...]
        rounded_ref[0:kept] = before[1][...]
    for code_ref, cut in zip(codes, cuts):
        devices, rows, width = code_ref.shape
        for begin, end in zip((0, *cut), (*cut, width)):
            total = jnp.zeros((rows, end - begin), jnp.float32)
            for d in range(devices):
                power = code_ref[d, :, begin : begin + LANES].astype(jnp.int32)[:, LANES - 1 : LANES]
                unit = 1.0 / (jnp.ones_like(power) << power).astype(jnp.float32)
                total += code_ref[d, :, begin:end].astype(jnp.int32).astype(jnp.float32) * unit
            lane = lax.broadcasted_iota(jnp.int32, total.shape, 1)
            total = jnp.where(lane == LANES - 1, 0.0, total) * live_ref[...]
            for n in range((end - begin) // LANES):
                part = total[:, n * LANES : (n + 1) * LANES]
                coef_ref[at] = part
                rounded_ref[at] = part.astype(jnp.bfloat16)
                at += 1


def collect(codes, live_rows, cuts=None, before=()):
    rows = codes[0].shape[1]
    kept = before[0].shape[0] if before else 0
    total = kept + sum(code.shape[2] // LANES for code in codes)
    cuts = cuts or [()] * len(codes)
    return pl.pallas_call(
        lambda *refs: collect_kernel(cuts, kept, *refs),
        in_specs=[IN_VMEM] * (1 + len(codes) + len(before)),
        out_specs=(IN_VMEM, IN_VMEM),
        out_shape=(
            jax.ShapeDtypeStruct((total, rows, LANES), jnp.float32),
            jax.ShapeDtypeStruct((total, rows, LANES), jnp.bfloat16),
        ),
        compiler_params=pltpu.CompilerParams(vmem_limit_bytes=12 * MEGA),
        name="collect",
    )(live_rows, *codes, *before)


def quad_kernel(groups, tables, ids_ref, own_ref, node_ref, pick_ref, *refs):
    coefs, refs = refs[:groups], refs[groups:]
    pieces, refs = refs[: groups * SIDE], refs[groups * SIDE :]
    weights, (out_ref, flat, store, sems) = refs[:tables], refs[tables:]
    rows = coefs[0].shape[1]
    blocks = out_ref.shape[0]
    for i, ref in enumerate(weights):
        count = ref.shape[0]
        pltpu.make_async_copy(ref, store.at[i * count : (i + 1) * count], sems.at[i]).start()
    at = 0
    for g in range(groups):
        for n in range(coefs[g].shape[0]):
            k = ids_ref[at]
            out_ref[k, 0:rows, :] = coefs[g][n]
            lane = pl.ds(pl.multiple_of(k * LANES, LANES), LANES)
            for d in range(SIDE):
                flat[d * rows : (d + 1) * rows, lane] = pieces[g * SIDE + d][n]
            at += 1
    right = flat[...]
    count = weights[0].shape[0]

    def add(i, total):
        pltpu.make_async_copy(store.at[0:count], store.at[pl.ds(i * count, count)], sems.at[i]).wait()
        lane = pl.ds(pl.multiple_of(own_ref[i] * LANES, LANES), LANES)
        left = flat[:, lane].astype(jnp.float32).T
        applied = lax.dot_general(
            store[pl.ds(i * count, count)].reshape(count * LANES, store.shape[2]),
            right,
            (((1,), (1,)), ((), ())),
            preferred_element_type=jnp.float32,
        )
        for n in range(count):
            value = jnp.sum(left * applied[n * LANES : (n + 1) * LANES], axis=0, keepdims=True)
            total += value * pick_ref[pl.ds(node_ref[i] + n, 1), :]
        return total

    total = lax.fori_loop(0, tables, add, jnp.zeros((1, SIDE * rows), jnp.float32))
    first = jnp.zeros((8, LANES), jnp.float32)
    line = lax.broadcasted_iota(jnp.int32, (8, LANES), 0)
    rest = jnp.concatenate([total[:, LANES:], jnp.zeros((1, 2 * LANES - SIDE * rows), jnp.float32)], axis=1)
    first = jnp.where(line == 0, total[:, 0:LANES], jnp.where(line == 1, rest, 0.0))
    for k in range(blocks):
        out_ref[k, rows : rows + 8, :] = first


def quadratic(ids, own, nodes_at, pick, coefs, pieces, weights):
    rows = coefs[0].shape[1]
    blocks = sum(c.shape[0] for c in coefs)
    return pl.pallas_call(
        lambda *refs: quad_kernel(len(coefs), len(weights), *refs),
        in_specs=[IN_SMEM] * 3 + [IN_VMEM] * (1 + len(coefs) + len(pieces)) + [IN_HBM] * len(weights),
        out_specs=IN_VMEM,
        out_shape=jax.ShapeDtypeStruct((blocks, rows + 8, LANES), jnp.float32),
        scratch_shapes=[
            pltpu.VMEM((SIDE * rows, blocks * LANES), jnp.bfloat16),
            pltpu.VMEM((sum(w.shape[0] for w in weights), LANES, blocks * LANES), jnp.bfloat16),
            pltpu.SemaphoreType.DMA((len(weights),)),
        ],
        compiler_params=pltpu.CompilerParams(vmem_limit_bytes=20 * MEGA),
        name="quad",
    )(ids, own, nodes_at, pick, *coefs, *pieces, *map(pin, weights))


def local(pair_density, eigvecs, subspace, counts, freq_index, band_weight):
    slots, states, depth = pair_density.shape
    nodes, share, neig = subspace.shape
    devices = lax.axis_size("gvec")
    bands = lax.axis_size("band")
    chips = bands // 2
    nrows = slots * states
    rows = nrows // devices
    band, gvec = lax.axis_index("band"), lax.axis_index("gvec")
    zed, core = band >> 1, band & 1
    why, ex = gvec >> 2, gvec & 3

    def shift(value, by):
        return lax.ppermute(value, "band", [(b, (b + 2 * by) % bands) for b in range(bands)])

    def sibling(value):
        return lax.ppermute(value, "band", [(b, b ^ 1) for b in range(bands)])

    def along_y(value, by):
        return lax.ppermute(value, "gvec", [(g, (g + SIDE * by) % devices) for g in range(devices)])

    def along_x(value):
        pairs = []
        for b in range(bands):
            for g in range(devices):
                to = g // SIDE * SIDE + (g + (1 if b % 2 == 0 else -1)) % SIDE
                pairs.append((b * devices + g, b * devices + to))
        return lax.ppermute(value, ("band", "gvec"), pairs)

    def along_z(value):
        return lax.ppermute(value, "band", [(b, (b + (2 if b % 2 == 0 else -2)) % bands) for b in range(bands)])

    flat = pair_density.reshape(nrows, depth)
    there, pair = 1 - core, nodes // 2
    turn = 2 * core - 1
    here, beside = core * pair, there * pair
    first_node = jnp.stack([here, beside]).astype(jnp.int32)
    nodes_at = jnp.stack([here, beside, here, beside, beside, here, here, beside]).astype(jnp.int32)
    x_at = [ex + d for d in (0, 0, turn, turn, -turn, -turn, 2, 2)]
    own = jnp.stack([why * SIDE + (x & (SIDE - 1)) for x in x_at]).astype(jnp.int32)

    steps = chips // 2
    places = [[zed]]
    for step in range(1, steps):
        places.append([(zed - step) & (chips - 1), (zed + step) & (chips - 1)])
    places.append([(zed + steps) & (chips - 1)])
    ids = []
    for begin, end in GROUPS:
        ids += [2 * z + c for step in range(begin, end) for z in places[step] for c in (core, there)]
    ids = jnp.stack(ids).astype(jnp.int32)


    def window(run, *operands):
        like = jax.eval_shape(run, *operands)
        return lax.cond(
            counts[0] > 0, run, lambda *_: jax.tree.map(lambda v: jnp.zeros(v.shape, v.dtype), like), *operands
        )

    def spread_rows(rounded):
        return [rounded] + [along_y(rounded, d) for d in range(1, SIDE)]

    def pair_up(blocks):
        return [part for block in blocks for part in (block, tuple(sibling(half) for half in block))]

    def send(code):
        return lax.all_to_all(code, "gvec", 0, 0)

    def first(flat, eigvecs, subspace, band_weight, freq_index):
        mine = jnp.pad(eigvecs, ((0, 0), (0, LANES - share)))
        up, down = shift(mine, 1), shift(mine, -1)
        table = spread(first_node, subspace)
        near = along_x(table[0])
        code = project(flat, pair_up([(mine,)]), devices)
        live = (jnp.arange(slots, dtype=jnp.int32) < counts[0]).astype(jnp.float32)
        live_rows = jnp.repeat(live, states).reshape(devices, rows, 1)
        weight_rows = jnp.repeat(band_weight * live, states).reshape(devices, rows)
        freq_rows = freq_index.reshape(devices, rows)
        order = [(((why - d) & (SIDE - 1)) * SIDE + ex) for d in range(SIDE)]
        freq_here = jnp.concatenate([lax.dynamic_index_in_dim(freq_rows, p, 0, False) for p in order])
        weight_here = jnp.concatenate([lax.dynamic_index_in_dim(weight_rows, p, 0, False) for p in order])
        pick = jnp.where(
            freq_here[None, :] == jnp.arange(nodes, dtype=jnp.int32)[:, None], weight_here[None, :], jnp.float32(0.0)
        )
        live_here = lax.dynamic_index_in_dim(live_rows, gvec, 0, False)

        return up, down, code, table, near, pick, live_here

    def middle(flat, up, down, code, rows_out):
        code_now = project(flat, pair_up([(up,), (down,)]), devices)
        return shift(up, 1), shift(down, -1), code_now, send(code), along_x(rows_out)

    def fourth(flat, up, down, code, landing, live_here):
        far = along_z(jnp.where(core == 0, up, down))
        coef, rounded = collect(landing, live_here)
        code_now = project(flat, pair_up([(up,), (down,)]), devices, room=2)
        return far, code_now, send(code), coef, spread_rows(rounded)

    def fifth(flat, far, code, landing, live_here, near, farther, across):
        swapped = [sibling(near), sibling(farther), sibling(across)]
        code = project(flat, pair_up([(far,)]), devices, into=code)
        return send(code), collect(landing, live_here), swapped

    def sixth(landing, live_here, before):
        coef, rounded = collect(landing, live_here, [(4 * LANES,)], before)
        return coef, spread_rows(rounded)

    up, down, code, table, near, pick, live_here = window(first, flat, eigvecs, subspace, band_weight, freq_index)
    up, down, code, landed_0, across = window(middle, flat, up, down, code, near)
    up, down, code, landed_1, farther = window(middle, flat, up, down, code, table[1])
    far, code, landed_2, coef_a, pieces_a = window(fourth, flat, up, down, code, [landed_0, landed_1], live_here)
    landed_3, before, swapped = window(fifth, flat, far, code, [landed_2], live_here, near, farther, across)
    coef_b, pieces_b = window(sixth, [landed_3], live_here, before)
    weights = [*table, near, farther, swapped[0], swapped[1], across, swapped[2]]
    coefs, pieces = [coef_a, coef_b], pieces_a + pieces_b
    message = quadratic(ids, own, nodes_at, pick, coefs, pieces, weights)
    landed = lax.all_to_all(message, "gvec", 0, 0)
    coef_out = landed[:, 0:rows, 0:share].reshape(slots, states, share)
    terms = jnp.sum(landed[:, rows : rows + 2, :], axis=0)
    terms = jnp.sum(terms.reshape(2 * LANES // states, states), axis=0)
    spread_terms = lax.all_to_all(jnp.broadcast_to(terms, (bands, states)), "band", 0, 0)
    total = jnp.sum(spread_terms, axis=0)
    scale_factor = math.sqrt(NEIG * bands * slots)
    sigma = -total / jnp.float32(scale_factor)
    return (coef_out, sigma)


def solution(mesh):
    in_specs = (
        P("band", None, "gvec"),
        P("gvec", "band"),
        P(None, "gvec", None),
        P("band"),
        P("band", None),
        P("band"),
    )
    out_specs = (P("band", None, "gvec"), P())
    return jax.shard_map(local, mesh=mesh, in_specs=in_specs, out_specs=out_specs, check_vma=False)
```

```python
import math

import jax
import jax.numpy as jnp
from jax import lax
from jax.experimental import pallas as pl
from jax.experimental.pallas import tpu as pltpu
from jax.sharding import PartitionSpec as P

NEIG = 2000
LANES = 128
LIMIT = 32000.0
STEPS = 24
SIDE = 4
GROUPS = ((0, 2), (2, 5))
SPLIT = 4
JOIN = 2
MEGA = 1024 * 1024
ANYWHERE = pl.BlockSpec(memory_space=pl.ANY)
IN_VMEM = pl.BlockSpec(memory_space=pltpu.VMEM)
IN_HBM = pl.BlockSpec(memory_space=pltpu.HBM)
IN_SMEM = pl.BlockSpec(memory_space=pltpu.SMEM)


def pin(value):
    return pltpu.with_memory_space_constraint(value, pltpu.HBM)


def spread_kernel(first_ref, w_ref, *outs):
    share = w_ref.shape[1]
    for side, ref in enumerate(outs):
        count, _, width = ref.shape
        ref[...] = jnp.zeros_like(ref)

        def one(n, carry, side=side, ref=ref):
            rows = w_ref[first_ref[side] + n]
            for k in range(width // LANES):
                ref[n, 0:share, k * LANES : k * LANES + share] = rows[:, k * share : (k + 1) * share]
            return carry

        lax.fori_loop(0, count, one, 0)


def spread(first, subspace):
    nodes, share, neig = subspace.shape
    half = jax.ShapeDtypeStruct((nodes // 2, LANES, neig // share * LANES), subspace.dtype)
    return pl.pallas_call(
        spread_kernel,
        in_specs=[IN_SMEM, IN_VMEM],
        out_specs=[IN_VMEM, IN_VMEM],
        out_shape=[half, half],
        compiler_params=pltpu.CompilerParams(vmem_limit_bytes=16 * MEGA),
        name="spread",
    )(first, subspace)


def project_kernel(shape, pd_ref, *refs):
    out_ref = refs[-1]
    at, columns = 0, []
    for count in shape:
        parts = [ref[...] for ref in refs[at : at + count]]
        columns.append(parts[0] if count == 1 else jnp.concatenate(parts, axis=0))
        at += count
    total = jnp.dot(pd_ref[...], jnp.concatenate(columns, axis=1), preferred_element_type=jnp.float32)
    most = jnp.max(jnp.abs(total), axis=1, keepdims=True)
    scale = jnp.ones_like(most)
    power = jnp.zeros(most.shape, jnp.int32)
    for j in range(1, STEPS + 1):
        fits = most * float(2**j) <= LIMIT
        scale = jnp.where(fits, float(2**j), scale)
        power = jnp.where(fits, j, power)
    code = jnp.round(total * scale).astype(jnp.int32)
    lane = lax.broadcasted_iota(jnp.int32, code.shape, 1)
    code = jnp.where(lane == LANES - 1, power, code).astype(jnp.int16)
    out_ref[...] = code.reshape(out_ref.shape)


def project(flat, blocks, devices, room=0, into=None):
    nrows, depth = flat.shape
    share = nrows // devices
    shape = [len(block) for block in blocks]
    parts = [part for block in blocks for part in block]
    width = len(blocks) * LANES
    whole = width + room * LANES if into is None else into.shape[2]
    place = 0 if into is None else whole // width - 1
    extra = () if into is None else (into,)
    return pl.pallas_call(
        lambda pd_ref, *refs: project_kernel(shape, pd_ref, *refs[: len(parts)], refs[-1]),
        grid=(SPLIT,),
        in_specs=[pl.BlockSpec((nrows // SPLIT, depth), lambda i: (i, 0))]
        + [pl.BlockSpec(part.shape, lambda i: (0, 0)) for part in parts]
        + [ANYWHERE] * len(extra),
        out_specs=pl.BlockSpec((devices // SPLIT, share, width), lambda i: (i, 0, place)),
        out_shape=pltpu.HBM((devices, share, whole), jnp.int16),
        input_output_aliases={1 + len(parts): 0} if extra else {},
        compiler_params=pltpu.CompilerParams(vmem_limit_bytes=32 * MEGA),
        cost_estimate=pl.CostEstimate(flops=10**6, bytes_accessed=10**4, transcendentals=0),
        name="project",
    )(pin(flat), *parts, *map(pin, extra))


def collect_kernel(cuts, kept, live_ref, *refs):
    codes, before, coef_ref, rounded_ref = refs[: len(cuts)], refs[len(cuts) : -2], refs[-2], refs[-1]
    at = kept
    if kept:
        coef_ref[0:kept] = before[0][...]
        rounded_ref[0:kept] = before[1][...]
    for code_ref, cut in zip(codes, cuts):
        devices, rows, width = code_ref.shape
        for begin, end in zip((0, *cut), (*cut, width)):
            total = jnp.zeros((rows, end - begin), jnp.float32)
            for d in range(devices):
                power = code_ref[d, :, begin : begin + LANES].astype(jnp.int32)[:, LANES - 1 : LANES]
                unit = 1.0 / (jnp.ones_like(power) << power).astype(jnp.float32)
                total += code_ref[d, :, begin:end].astype(jnp.int32).astype(jnp.float32) * unit
            lane = lax.broadcasted_iota(jnp.int32, total.shape, 1)
            total = jnp.where(lane == LANES - 1, 0.0, total) * live_ref[...]
            for n in range((end - begin) // LANES):
                part = total[:, n * LANES : (n + 1) * LANES]
                coef_ref[at] = part
                rounded_ref[at] = part.astype(jnp.bfloat16)
                at += 1


def collect(codes, live_rows, cuts=None, before=()):
    rows = codes[0].shape[1]
    kept = before[0].shape[0] if before else 0
    total = kept + sum(code.shape[2] // LANES for code in codes)
    cuts = cuts or [()] * len(codes)
    return pl.pallas_call(
        lambda *refs: collect_kernel(cuts, kept, *refs),
        in_specs=[IN_VMEM] * (1 + len(codes) + len(before)),
        out_specs=(IN_VMEM, IN_VMEM),
        out_shape=(
            jax.ShapeDtypeStruct((total, rows, LANES), jnp.float32),
            jax.ShapeDtypeStruct((total, rows, LANES), jnp.bfloat16),
        ),
        compiler_params=pltpu.CompilerParams(vmem_limit_bytes=12 * MEGA),
        name="collect",
    )(live_rows, *codes, *before)


def quad_kernel(groups, tables, ids_ref, own_ref, node_ref, pick_ref, *refs):
    coefs, refs = refs[:groups], refs[groups:]
    pieces, refs = refs[: groups * SIDE], refs[groups * SIDE :]
    weights, (out_ref, flat, store, sems) = refs[:tables], refs[tables:]
    rows = coefs[0].shape[1]
    blocks = out_ref.shape[0]
    for i, ref in enumerate(weights):
        count = ref.shape[0]
        pltpu.make_async_copy(ref, store.at[i * count : (i + 1) * count], sems.at[i]).start()
    at = 0
    for g in range(groups):
        for n in range(coefs[g].shape[0]):
            k = ids_ref[at]
            out_ref[k, 0:rows, :] = coefs[g][n]
            lane = pl.ds(pl.multiple_of(k * LANES, LANES), LANES)
            for d in range(SIDE):
                flat[d * rows : (d + 1) * rows, lane] = pieces[g * SIDE + d][n]
            at += 1
    right = flat[...]
    count = weights[0].shape[0]

    def add(step, total):
        span = pl.ds(step * JOIN * count, JOIN * count)
        for j in range(JOIN):
            i = step * JOIN + j
            pltpu.make_async_copy(store.at[0:count], store.at[pl.ds(i * count, count)], sems.at[i]).wait()
        applied = lax.dot_general(
            store[span].reshape(JOIN * count * LANES, store.shape[2]),
            right,
            (((1,), (1,)), ((), ())),
            preferred_element_type=jnp.float32,
        )
        for j in range(JOIN):
            i = step * JOIN + j
            lane = pl.ds(pl.multiple_of(own_ref[i] * LANES, LANES), LANES)
            left = flat[:, lane].astype(jnp.float32).T
            for n in range(count):
                part = applied[(j * count + n) * LANES : (j * count + n + 1) * LANES]
                value = jnp.sum(left * part, axis=0, keepdims=True)
                total += value * pick_ref[pl.ds(node_ref[i] + n, 1), :]
        return total

    total = lax.fori_loop(0, tables // JOIN, add, jnp.zeros((1, SIDE * rows), jnp.float32))
    first = jnp.zeros((8, LANES), jnp.float32)
    line = lax.broadcasted_iota(jnp.int32, (8, LANES), 0)
    rest = jnp.concatenate([total[:, LANES:], jnp.zeros((1, 2 * LANES - SIDE * rows), jnp.float32)], axis=1)
    first = jnp.where(line == 0, total[:, 0:LANES], jnp.where(line == 1, rest, 0.0))
    for k in range(blocks):
        out_ref[k, rows : rows + 8, :] = first


def quadratic(ids, own, nodes_at, pick, coefs, pieces, weights):
    rows = coefs[0].shape[1]
    blocks = sum(c.shape[0] for c in coefs)
    return pl.pallas_call(
        lambda *refs: quad_kernel(len(coefs), len(weights), *refs),
        in_specs=[IN_SMEM] * 3 + [IN_VMEM] * (1 + len(coefs) + len(pieces)) + [IN_HBM] * len(weights),
        out_specs=IN_VMEM,
        out_shape=jax.ShapeDtypeStruct((blocks, rows + 8, LANES), jnp.float32),
        scratch_shapes=[
            pltpu.VMEM((SIDE * rows, blocks * LANES), jnp.bfloat16),
            pltpu.VMEM((sum(w.shape[0] for w in weights), LANES, blocks * LANES), jnp.bfloat16),
            pltpu.SemaphoreType.DMA((len(weights),)),
        ],
        compiler_params=pltpu.CompilerParams(vmem_limit_bytes=20 * MEGA),
        name="quad",
    )(ids, own, nodes_at, pick, *coefs, *pieces, *map(pin, weights))


def local(pair_density, eigvecs, subspace, counts, freq_index, band_weight):
    slots, states, depth = pair_density.shape
    nodes, share, neig = subspace.shape
    devices = lax.axis_size("gvec")
    bands = lax.axis_size("band")
    chips = bands // 2
    nrows = slots * states
    rows = nrows // devices
    band, gvec = lax.axis_index("band"), lax.axis_index("gvec")
    zed, core = band >> 1, band & 1
    why, ex = gvec >> 2, gvec & 3

    def shift(value, by):
        return lax.ppermute(value, "band", [(b, (b + 2 * by) % bands) for b in range(bands)])

    def sibling(value):
        return lax.ppermute(value, "band", [(b, b ^ 1) for b in range(bands)])

    def along_y(value, by):
        return lax.ppermute(value, "gvec", [(g, (g + SIDE * by) % devices) for g in range(devices)])

    def along_x(value):
        pairs = []
        for b in range(bands):
            for g in range(devices):
                to = g // SIDE * SIDE + (g + (1 if b % 2 == 0 else -1)) % SIDE
                pairs.append((b * devices + g, b * devices + to))
        return lax.ppermute(value, ("band", "gvec"), pairs)

    def along_z(value):
        return lax.ppermute(value, "band", [(b, (b + (2 if b % 2 == 0 else -2)) % bands) for b in range(bands)])

    flat = pair_density.reshape(nrows, depth)
    there, pair = 1 - core, nodes // 2
    turn = 2 * core - 1
    here, beside = core * pair, there * pair
    first_node = jnp.stack([here, beside]).astype(jnp.int32)
    nodes_at = jnp.stack([here, beside, here, beside, beside, here, here, beside]).astype(jnp.int32)
    x_at = [ex + d for d in (0, 0, turn, turn, -turn, -turn, 2, 2)]
    own = jnp.stack([why * SIDE + (x & (SIDE - 1)) for x in x_at]).astype(jnp.int32)

    steps = chips // 2
    places = [[zed]]
    for step in range(1, steps):
        places.append([(zed - step) & (chips - 1), (zed + step) & (chips - 1)])
    places.append([(zed + steps) & (chips - 1)])
    ids = []
    for begin, end in GROUPS:
        ids += [2 * z + c for step in range(begin, end) for z in places[step] for c in (core, there)]
    ids = jnp.stack(ids).astype(jnp.int32)


    def window(run, *operands):
        like = jax.eval_shape(run, *operands)
        return lax.cond(
            counts[0] > 0, run, lambda *_: jax.tree.map(lambda v: jnp.zeros(v.shape, v.dtype), like), *operands
        )

    def spread_rows(rounded):
        return [rounded] + [along_y(rounded, d) for d in range(1, SIDE)]

    def pair_up(blocks):
        return [part for block in blocks for part in (block, tuple(sibling(half) for half in block))]

    def send(code):
        return lax.all_to_all(code, "gvec", 0, 0)

    def first(flat, eigvecs, subspace, band_weight, freq_index):
        mine = jnp.pad(eigvecs, ((0, 0), (0, LANES - share)))
        up, down = shift(mine, 1), shift(mine, -1)
        table = spread(first_node, subspace)
        near = along_x(table[0])
        code = project(flat, pair_up([(mine,)]), devices)
        live = (jnp.arange(slots, dtype=jnp.int32) < counts[0]).astype(jnp.float32)
        live_rows = jnp.repeat(live, states).reshape(devices, rows, 1)
        weight_rows = jnp.repeat(band_weight * live, states).reshape(devices, rows)
        freq_rows = freq_index.reshape(devices, rows)
        order = [(((why - d) & (SIDE - 1)) * SIDE + ex) for d in range(SIDE)]
        freq_here = jnp.concatenate([lax.dynamic_index_in_dim(freq_rows, p, 0, False) for p in order])
        weight_here = jnp.concatenate([lax.dynamic_index_in_dim(weight_rows, p, 0, False) for p in order])
        pick = jnp.where(
            freq_here[None, :] == jnp.arange(nodes, dtype=jnp.int32)[:, None], weight_here[None, :], jnp.float32(0.0)
        )
        live_here = lax.dynamic_index_in_dim(live_rows, gvec, 0, False)

        return up, down, code, table, near, pick, live_here

    def middle(flat, up, down, code, rows_out):
        code_now = project(flat, pair_up([(up,), (down,)]), devices)
        return shift(up, 1), shift(down, -1), code_now, send(code), along_x(rows_out)

    def fourth(flat, up, down, code, landing, live_here):
        far = along_z(jnp.where(core == 0, up, down))
        coef, rounded = collect(landing, live_here)
        code_now = project(flat, pair_up([(up,), (down,)]), devices, room=2)
        return far, code_now, send(code), coef, spread_rows(rounded)

    def fifth(flat, far, code, landing, live_here, near, farther, across):
        swapped = [sibling(near), sibling(farther), sibling(across)]
        code = project(flat, pair_up([(far,)]), devices, into=code)
        return send(code), collect(landing, live_here), swapped

    def sixth(landing, live_here, before):
        coef, rounded = collect(landing, live_here, [(4 * LANES,)], before)
        return coef, spread_rows(rounded)

    up, down, code, table, near, pick, live_here = window(first, flat, eigvecs, subspace, band_weight, freq_index)
    up, down, code, landed_0, across = window(middle, flat, up, down, code, near)
    up, down, code, landed_1, farther = window(middle, flat, up, down, code, table[1])
    far, code, landed_2, coef_a, pieces_a = window(fourth, flat, up, down, code, [landed_0, landed_1], live_here)
    landed_3, before, swapped = window(fifth, flat, far, code, [landed_2], live_here, near, farther, across)
    coef_b, pieces_b = window(sixth, [landed_3], live_here, before)
    weights = [*table, near, farther, swapped[0], swapped[1], across, swapped[2]]
    coefs, pieces = [coef_a, coef_b], pieces_a + pieces_b
    message = quadratic(ids, own, nodes_at, pick, coefs, pieces, weights)
    landed = lax.all_to_all(message, "gvec", 0, 0)
    coef_out = landed[:, 0:rows, 0:share].reshape(slots, states, share)
    terms = jnp.sum(landed[:, rows : rows + 2, :], axis=0)
    terms = jnp.sum(terms.reshape(2 * LANES // states, states), axis=0)
    spread_terms = lax.all_to_all(jnp.broadcast_to(terms, (bands, states)), "band", 0, 0)
    total = jnp.sum(spread_terms, axis=0)
    scale_factor = math.sqrt(NEIG * bands * slots)
    sigma = -total / jnp.float32(scale_factor)
    return (coef_out, sigma)


def solution(mesh):
    in_specs = (
        P("band", None, "gvec"),
        P("gvec", "band"),
        P(None, "gvec", None),
        P("band"),
        P("band", None),
        P("band"),
    )
    out_specs = (P("band", None, "gvec"), P())
    return jax.shard_map(local, mesh=mesh, in_specs=in_specs, out_specs=out_specs, check_vma=False)
```
